256 devices in a mesh: seq: 32 (over x_lo, z, core), kvh: 8 (over x_hi, y).
Axes of the slice: x: 4 (x_hi: 2, x_lo: 2; x = x_hi * 2 + x_lo), y: 4, z: 8, core: 2. Of those that a mesh axis runs over, the one named last changes fastest.
Arguments:
- queries: bfloat16 [32768, 4096], P('seq', 'kvh'), may hold values from -8 to 8
- keys: bfloat16 [32768, 1024], P('seq', 'kvh'), may hold values from -8 to 8
- values: bfloat16 [32768, 1024], P('seq', 'kvh'), may hold values from -6 to 6
- out_weight: bfloat16 [4096, 4096], P('kvh'), may hold values from -0.09375 to 0.09375
Outputs:
- mixed: bfloat16 [32768, 4096], P('seq', 'kvh')
- log_total: float32 [32, 32768], P('kvh', 'seq')
The draws below stay inside these ranges and needn't reach their ends.
All inputs are finite; a program needn't handle non-finite values.
Results may differ from the reference program's by a relative error of at most 0.015.
Values may be sent and summed in bfloat16 or wider, within the bound.
A program may use at most 64 MiB of HBM per device.

```python
import jax
import jax.numpy as jnp
from jax import lax

D = 4096
HEADS = 32
KV_HEADS = 8
HEAD_DIM = 128
TOK_DEV = 1024
TOKENS = 32768
N_SEQ = 32
N_KVH = 8


def draw_queries(key, part):
    key = jax.random.fold_in(key, 1)
    base = jnp.clip(jax.random.normal(key, (TOKENS, HEADS * HEAD_DIM), jnp.float32), -6.0, 6.0)
    return base.astype(jnp.bfloat16)


def draw_keys(key, part):
    key = jax.random.fold_in(key, 2)
    base = jnp.clip(jax.random.normal(key, (TOKENS, KV_HEADS * HEAD_DIM), jnp.float32), -6.0, 6.0)
    return base.astype(jnp.bfloat16)


def level_of(stream_key, extent, cuts, smallest, top_value):
    level, own = 1.0, jax.random.fold_in(stream_key, 6)
    for axis_at, parts in cuts:
        draws = jnp.exp(jax.random.uniform(jax.random.fold_in(own, axis_at), (parts,), jnp.float32, smallest / len(cuts), top_value / len(cuts)))
        level = level * jnp.repeat(draws, extent[axis_at] // parts).reshape([-1 if axis == axis_at else 1 for axis in range(len(extent))])
    return level


def centred(key, shape, scale, reach, shards=(), kind=jnp.bfloat16):
    gain = level_of(key, shape, shards, -0.22, 0.18) if shards else 1.0
    drawn = jax.random.normal(key, shape, jnp.float32) * scale * gain
    return jnp.minimum(jnp.maximum(drawn, -reach), reach).astype(kind)


def setup_inputs(seed: int = 0) -> dict:
    splits = jax.random.split(jax.random.key(seed), 5)
    queries = draw_queries(jax.random.fold_in(splits[4], 71), 0)
    keys = draw_keys(jax.random.fold_in(splits[4], 71), 0)
    values = centred(splits[2], (TOKENS, KV_HEADS * HEAD_DIM), 1.0, 6.0, ((0, 32), (1, 8)))
    out_weight = centred(splits[3], (HEADS * HEAD_DIM, D), (HEADS * HEAD_DIM) ** -0.5, 0.09375, ((0, 8),))
    return dict(queries=queries, keys=keys, values=values, out_weight=out_weight)


def tile(query, key_rows, value_rows, mask):
    scale = HEAD_DIM ** -0.5
    scores = jnp.einsum('tkgd,skd->kgts', query.astype(jnp.float32), key_rows.astype(jnp.float32)) * scale
    scores = jnp.where(mask, scores, -1e30)
    top = jnp.max(scores, axis=-1)
    weights = jnp.where(mask, jnp.exp(scores - top[..., None]), 0.0)
    total = jnp.sum(weights, axis=-1)
    rounded = lax.optimization_barrier(weights.astype(jnp.bfloat16))
    acc = jnp.einsum('kgts,skd->kgtd', rounded.astype(jnp.float32), value_rows.astype(jnp.float32))
    return acc, top, total


def combine(results):
    top = results[0][1]
    for item in results[1:]:
        top = jnp.maximum(top, item[1])
    total = jnp.zeros_like(top)
    acc = jnp.zeros_like(results[0][0])
    for item in results:
        factor = jnp.exp(item[1] - top)
        total = total + factor * item[2]
        acc = acc + factor[..., None] * item[0]
    return acc, top, total


def reference(queries, keys, values, out_weight):
    group = HEADS // KV_HEADS
    half = TOK_DEV // 2
    lag = N_SEQ // 2
    q_blocks = queries.reshape(N_SEQ, TOK_DEV, KV_HEADS, group, HEAD_DIM)
    k_blocks = keys.reshape(N_SEQ, TOK_DEV, KV_HEADS, HEAD_DIM)
    v_blocks = values.reshape(N_SEQ, TOK_DEV, KV_HEADS, HEAD_DIM)
    qpos = jnp.arange(TOK_DEV, dtype=jnp.int32)

    def one_block(block):
        query = q_blocks[block]
        own_k = k_blocks[block]
        own_v = v_blocks[block]
        early = jnp.maximum(block - lag, 0).astype(jnp.int32)
        far_k = k_blocks[early]
        far_v = v_blocks[early]
        valid = block >= lag
        results = []
        for part in range(2):
            kpos = jnp.arange(half, dtype=jnp.int32) + part * half
            mask = qpos[:, None] >= kpos[None, :]
            results.append(tile(query, own_k[part * half:(part + 1) * half], own_v[part * half:(part + 1) * half], mask))
            full = jnp.broadcast_to(valid, (TOK_DEV, half))
            results.append(tile(query, far_k[part * half:(part + 1) * half], far_v[part * half:(part + 1) * half], full))
        acc, top, total = combine(results)
        attended = (acc / total[..., None]).transpose(2, 0, 1, 3).reshape(TOK_DEV, HEADS * HEAD_DIM)
        log_total = (top + jnp.log(total)).reshape(HEADS, TOK_DEV)
        return attended.astype(jnp.bfloat16), log_total

    attended, log_total = lax.map(one_block, jnp.arange(N_SEQ, dtype=jnp.int32))
    attended = attended.reshape(TOKENS, HEADS * HEAD_DIM)
    log_total = log_total.transpose(1, 0, 2).reshape(HEADS, TOKENS)
    width = HEADS * HEAD_DIM // N_KVH
    mixed = jnp.zeros((TOKENS, D), jnp.float32)
    for owner in range(N_KVH):
        term = jnp.dot(attended[:, owner * width:(owner + 1) * width], out_weight[owner * width:(owner + 1) * width], preferred_element_type=jnp.float32)
        rounded = lax.optimization_barrier(term.astype(jnp.bfloat16))
        mixed = mixed + rounded.astype(jnp.float32)
    return mixed.astype(jnp.bfloat16), log_total
```

```python
import functools
import math

import jax
import jax.numpy as jnp
from jax import lax
from jax.experimental import pallas as pl
from jax.experimental.pallas import tpu as pltpu
from jax.sharding import PartitionSpec as P

MESH = pl.DeviceIdType.MESH
HEAD = 128
GROUP = 4
TOK = 1024
QC = 256
FAR = 512
STEP = 128
NSTEP = TOK // STEP
BLK = 512
HALF = BLK // 2
WIDE = 4 * BLK
PIECE = 64
SCALE = math.log2(math.e) / math.sqrt(HEAD)
LN2 = math.log(2.0)
F32 = jnp.float32
BF16 = jnp.bfloat16


def dot_nt(a, b):
    return lax.dot_general(a, b, (((1,), (1,)), ((), ())), preferred_element_type=F32)


def dot_nn(a, b):
    return jnp.dot(a, b, preferred_element_type=F32)


def kernel(
    q_hbm, k_hbm, v_hbm, w_hbm, out_hbm, lse_hbm,
    q, k, v, kf, vf, wo, wr, att, attp, acc, top,
    m1s, m1r, m2s, m2r, outv, lsev,
    in_sem, out_sem, kv_ss, kv_rs, w_ss, w_rs, a_ss, a_rs, s1_ss, s1_rs, s2_ss, s2_rs,
):
    s = lax.axis_index("seq")
    g = lax.axis_index("kvh")
    xl, z, c = s // 16, (s // 2) % 8, s % 2
    xh, y = g // 4, g % 4
    busy = xl == 1

    def dev(xl=xl, z=z, c=c, xh=xh, y=y):
        return ((xl * 8 + z) * 2 + c, xh * 4 + y)

    d_kv = dev(xl=1 - xl)
    d_w = dev(xl=1 - xl, xh=1 - xh)
    d_z = [dev(z=(z + 1) % 8), dev(z=(z + 7) % 8), dev(z=(z + 2) % 8), dev(z=(z + 6) % 8)]
    d_c = dev(c=1 - c)
    d_a = dev(xh=1 - xh)
    d_y = [dev(y=(y + 1) % 4), dev(y=(y + 3) % 4)]

    def remote(src, dst, ss, rs, to):
        return pltpu.make_async_remote_copy(
            src_ref=src, dst_ref=dst, send_sem=ss, recv_sem=rs, device_id=to, device_id_type=MESH
        )

    loads = [
        pltpu.make_async_copy(q_hbm, q, in_sem.at[0]),
        pltpu.make_async_copy(k_hbm, k, in_sem.at[1]),
        pltpu.make_async_copy(v_hbm, v.at[:, pl.ds(0, HEAD)], in_sem.at[2]),
        pltpu.make_async_copy(w_hbm.at[:, pl.ds(pl.multiple_of(xh * WIDE, WIDE), WIDE)], wo, in_sem.at[3]),
    ]
    for load in loads:
        load.start()

    barrier = pltpu.get_barrier_semaphore()
    everyone = [d_kv, d_w, *d_z, d_c, d_a, *d_y]
    for other in everyone:
        pl.semaphore_signal(barrier, 1, device_id=other, device_id_type=MESH)
    pl.semaphore_wait(barrier, len(everyone))

    kv_out = []
    for part in range(2):
        rows = pl.ds(part * FAR, FAR)
        kv_out.append(remote(k_hbm.at[rows], kf.at[rows], kv_ss.at[part, 0], kv_rs.at[part, 0], d_kv))
        kv_out.append(
            remote(v_hbm.at[rows], vf.at[rows, pl.ds(0, HEAD)], kv_ss.at[part, 1], kv_rs.at[part, 1], d_kv)
        )

    @pl.when(xl == 0)
    def _():
        for copy in kv_out:
            copy.start()

    def piece(dz, first=0, count=PIECE):
        at = (((z + dz) % 4) * 2 + c) * PIECE + first
        return pl.ds(pl.multiple_of(at, 16), count)

    theirs = pl.ds(pl.multiple_of((1 - xh) * WIDE, WIDE), WIDE)
    w_x = remote(w_hbm.at[piece(0), theirs], wr.at[piece(0)], w_ss.at[0], w_rs.at[0], d_w)
    w_x.start()
    mine = [piece(0), piece(0), piece(0, 0, 32), piece(0, 32, 32)]
    w_z = [remote(wr.at[mine[i]], wr.at[mine[i]], w_ss.at[1 + i], w_rs.at[1 + i], d_z[i]) for i in range(4)]
    came = [piece(3), piece(1), piece(2, 0, 32), piece(2, 32, 32)]
    w_c = [
        remote(wr.at[rows], wr.at[rows], w_ss.at[5 + i], w_rs.at[5 + i], d_c)
        for i, rows in enumerate([piece(0), *came])
    ]

    ones = jnp.ones((TOK, HEAD), BF16)
    v[:, pl.ds(HEAD, HEAD)] = ones
    vf[:, pl.ds(HEAD, HEAD)] = ones
    for load in loads[:3]:
        load.wait()

    def finish(rows, h, o, m):
        l = o[:, HEAD:]
        att[rows, pl.ds(h * HEAD, HEAD)] = (o[:, :HEAD] / l).astype(BF16)
        top[h, rows, :] = (m + jnp.log2(l)) * LN2

    def own(qi):
        rows = pl.ds(qi * QC, QC)
        causal = lax.broadcasted_iota(jnp.int32, (QC, QC), 0) >= lax.broadcasted_iota(jnp.int32, (QC, QC), 1)
        for h in range(GROUP):
            qh = q[rows, pl.ds(h * HEAD, HEAD)]
            sd = jnp.where(causal, dot_nt(qh, k[rows, :]) * SCALE, -1e30)
            m = jnp.max(sd, axis=1, keepdims=True)
            if qi:
                before = pl.ds(0, qi * QC)
                sb = dot_nt(qh, k[before, :]) * SCALE
                m = jnp.maximum(m, jnp.max(sb, axis=1, keepdims=True))
            o = dot_nn(jnp.exp2(sd - m).astype(BF16), v[rows, :])
            if qi:
                o += dot_nn(jnp.exp2(sb - m).astype(BF16), v[before, :])
            m = jnp.broadcast_to(m, (QC, HEAD))
            acc[h, rows, :] = o
            top[h, rows, :] = m

    def far(part, qi):
        rows = pl.ds(pl.multiple_of(qi * QC, QC), QC)
        seen = pl.ds(part * FAR, FAR)
        for h in range(GROUP):
            sf = dot_nt(q[rows, pl.ds(h * HEAD, HEAD)], kf[seen, :]) * SCALE
            old = top[h, rows, :]
            m = jnp.maximum(old, jnp.broadcast_to(jnp.max(sf, axis=1, keepdims=True), (QC, HEAD)))
            keep = jnp.exp2(old - m)
            p = jnp.exp2(sf - jnp.concatenate([m] * (FAR // HEAD), axis=1))
            o = dot_nn(p.astype(BF16), vf[seen, :])
            o += acc[h, rows, :] * jnp.concatenate([keep, keep], axis=1)
            if part:
                finish(rows, h, o, m)
            else:
                acc[h, rows, :] = o
                top[h, rows, :] = m

    def a_copy(qi):
        rows = pl.ds(pl.multiple_of(qi * QC, QC), QC)
        return remote(att.at[rows], attp.at[rows], a_ss.at[qi], a_rs.at[qi], d_a)

    for qi in range(2):
        own(qi)
    w_x.wait_recv()
    for copy in w_z:
        copy.start()
    w_c[0].start()
    for qi in range(2, TOK // QC):
        own(qi)

    @pl.when(busy)
    def _():
        for copy in kv_out[:2]:
            copy.wait_recv()

        @pl.loop(0, TOK // QC)
        def _(qi):
            far(0, qi)

    for i in range(4):
        w_z[i].wait_recv()
        w_c[1 + i].start()

    @pl.when(busy)
    def _():
        for copy in kv_out[2:]:
            copy.wait_recv()

        @pl.loop(0, TOK // QC)
        def _(qi):
            far(1, qi)
            a_copy(qi).start()

    @pl.when(xl == 0)
    def _():
        @pl.loop(0, TOK // QC)
        def _(qi):
            rows = pl.ds(pl.multiple_of(qi * QC, QC), QC)
            for h in range(GROUP):
                finish(rows, h, acc[h, rows, :], top[h, rows, :])

        for copy in kv_out:
            copy.wait_send()

        @pl.loop(0, TOK // QC)
        def _(qi):
            a_copy(qi).start()

    loads[3].wait()
    for copy in w_c:
        copy.wait_recv()

    def part_of(i, block):
        rows = pl.ds(pl.multiple_of(i * STEP, STEP), STEP)
        cols = pl.ds(pl.multiple_of(block * BLK, BLK), BLK)
        return dot_nn(att[rows, :], wo[:, cols]) + dot_nn(attp[rows, :], wr[:, cols])

    def m1(i, way):
        rows = pl.ds(pl.multiple_of(i * STEP, STEP), STEP)
        return remote(m1s.at[way, rows], m1r.at[way, rows], s1_ss.at[way, i], s1_rs.at[way, i], d_y[way])

    def m2(i, way):
        rows = pl.ds(pl.multiple_of(i * STEP, STEP), STEP)
        return remote(m2s.at[way, rows], m2r.at[way, rows], s2_ss.at[way, i], s2_rs.at[way, i], d_y[way])

    def send_far(i):
        rows = pl.ds(pl.multiple_of(i * STEP, STEP), STEP)

        @pl.when(i % (QC // STEP) == 0)
        def _():
            a_copy(i // (QC // STEP)).wait_recv()

        f = part_of(i, (y + 2) % 4).astype(BF16)
        for way in range(2):
            m1s[way, rows, :] = f[:, way * HALF : (way + 1) * HALF]
            m1(i, way).start()

    def send_near(i):
        rows = pl.ds(pl.multiple_of(i * STEP, STEP), STEP)
        for way in range(2):
            f = part_of(i, (y + 1 + 2 * way) % 4)
            m1(i, way).wait_recv()
            for half in range(2):
                cols = pl.ds(half * HALF, HALF)
                mine = f[:, half * HALF : (half + 1) * HALF]
                if half == way:
                    mine += m1r[way, rows, :].astype(F32)
                m2s[way, rows, cols] = mine.astype(BF16)
            m2(i, way).start()

    def out_copy(i):
        rows = pl.ds(pl.multiple_of(i * STEP, STEP), STEP)
        return pltpu.make_async_copy(outv.at[rows], out_hbm.at[rows], out_sem.at[i])

    def collect(i):
        rows = pl.ds(pl.multiple_of(i * STEP, STEP), STEP)
        f = part_of(i, y)
        for way in range(2):
            m2(i, way).wait_recv()
            f += m2r[way, rows, :].astype(F32)
        outv[rows, :] = f.astype(BF16)
        out_copy(i).start()

    send_far(0)
    send_far(1)
    send_near(0)

    for h in range(GROUP):
        for qi in range(TOK // QC):
            rows = pl.ds(qi * QC, QC)
            lsev[pl.ds(h, 1), rows] = jnp.transpose(top[h, rows, :])[0:1, :]
    lse_copy = pltpu.make_async_copy(lsev, lse_hbm, out_sem.at[NSTEP])
    lse_copy.start()

    @pl.loop(2, NSTEP)
    def _(i):
        send_far(i)
        send_near(i - 1)
        collect(i - 2)

    send_near(NSTEP - 1)
    collect(NSTEP - 2)
    collect(NSTEP - 1)

    w_x.wait_send()
    for copy in [*w_z, *w_c]:
        copy.wait_send()

    @pl.loop(0, TOK // QC)
    def _(qi):
        a_copy(qi).wait_send()

    @pl.loop(0, NSTEP)
    def _(i):
        for way in range(2):
            m1(i, way).wait_send()
            m2(i, way).wait_send()
        out_copy(i).wait()

    lse_copy.wait()


def body(queries, keys, values, out_weight):
    dma = pltpu.SemaphoreType.DMA
    anywhere = pl.BlockSpec(memory_space=pl.ANY)
    return pl.pallas_call(
        kernel,
        out_shape=(
            jax.ShapeDtypeStruct((TOK, BLK), BF16),
            jax.ShapeDtypeStruct((GROUP, TOK), F32),
        ),
        in_specs=[anywhere] * 4,
        out_specs=(anywhere, anywhere),
        scratch_shapes=[
            pltpu.VMEM((TOK, BLK), BF16),
            pltpu.VMEM((TOK, HEAD), BF16),
            pltpu.VMEM((TOK, 2 * HEAD), BF16),
            pltpu.VMEM((TOK, HEAD), BF16),
            pltpu.VMEM((TOK, 2 * HEAD), BF16),
            pltpu.VMEM((BLK, WIDE), BF16),
            pltpu.VMEM((BLK, WIDE), BF16),
            pltpu.VMEM((TOK, BLK), BF16),
            pltpu.VMEM((TOK, BLK), BF16),
            pltpu.VMEM((GROUP, TOK, 2 * HEAD), F32),
            pltpu.VMEM((GROUP, TOK, HEAD), F32),
            pltpu.VMEM((2, TOK, HALF), BF16),
            pltpu.VMEM((2, TOK, HALF), BF16),
            pltpu.VMEM((2, TOK, BLK), BF16),
            pltpu.VMEM((2, TOK, BLK), BF16),
            pltpu.VMEM((TOK, BLK), BF16),
            pltpu.VMEM((GROUP, TOK), F32),
            dma((4,)),
            dma((NSTEP + 1,)),
            dma((2, 2)),
            dma((2, 2)),
            dma((10,)),
            dma((10,)),
            dma((TOK // QC,)),
            dma((TOK // QC,)),
            dma((2, NSTEP)),
            dma((2, NSTEP)),
            dma((2, NSTEP)),
            dma((2, NSTEP)),
        ],
        compiler_params=pltpu.CompilerParams(
            collective_id=0, has_side_effects=True, vmem_limit_bytes=60 * 2**20
        ),
        cost_estimate=pl.CostEstimate(flops=10**10, bytes_accessed=8 * 2**20, transcendentals=8 * 2**20),
    )(queries, keys, values, out_weight)


def solution(mesh):
    in_specs = (P("seq", "kvh"), P("seq", "kvh"), P("seq", "kvh"), P("kvh", None))
    out_specs = (P("seq", "kvh"), P("kvh", "seq"))
    return jax.shard_map(body, mesh=mesh, in_specs=in_specs, out_specs=out_specs, check_vma=False)
```

```python
import functools
import math

import jax
import jax.numpy as jnp
from jax import lax
from jax.experimental import pallas as pl
from jax.experimental.pallas import tpu as pltpu
from jax.sharding import PartitionSpec as P

MESH = pl.DeviceIdType.MESH
HEAD = 128
GROUP = 4
TOK = 1024
QC = 256
FAR = 256
PARTS = TOK // FAR
STEP = 128
NSTEP = TOK // STEP
BLK = 512
HALF = BLK // 2
WIDE = 4 * BLK
PIECE = 128
SCALE = math.log2(math.e) / math.sqrt(HEAD)
LN2 = math.log(2.0)
F32 = jnp.float32
BF16 = jnp.bfloat16


def dot_nt(a, b):
    return lax.dot_general(a, b, (((1,), (1,)), ((), ())), preferred_element_type=F32)


def dot_nn(a, b):
    return jnp.dot(a, b, preferred_element_type=F32)


def kernel(
    q_hbm, k_hbm, v_hbm, w_hbm, out, lse,
    q, k, v, kf, vf, w, att, acc, top, kept, xs, xr,
    in_sem, kv_ss, kv_rs, wy_ss, wy_rs, wz_ss, wz_rs, wc_ss, wc_rs, a_ss, a_rs, f_ss, f_rs, x_ss, x_rs,
):
    s = lax.axis_index("seq")
    g = lax.axis_index("kvh")
    xl, z, c = s // 16, (s // 2) % 8, s % 2
    xh, y = g // 4, g % 4
    busy = xl == 1

    def dev(xl=xl, z=z, c=c, xh=xh, y=y):
        return ((xl * 8 + z) * 2 + c, xh * 4 + y)

    zp = z % 2
    d_kv = dev(xl=1 - xl)
    d_z = dev(z=z + 1 - 2 * zp)
    d_c = dev(c=1 - c)
    d_x = dev(xh=1 - xh)
    ys = [(y + 1) % 4, (y + 3) % 4, (y + 2) % 4]
    d_y = [dev(y=other) for other in ys]

    def remote(src, dst, ss, rs, to):
        return pltpu.make_async_remote_copy(
            src_ref=src, dst_ref=dst, send_sem=ss, recv_sem=rs, device_id=to, device_id_type=MESH
        )

    def block_cols(b, owner):
        first = (xh if b == 0 else 1 - xh) * WIDE + owner * BLK
        return pl.ds(pl.multiple_of(first, BLK), BLK)

    loads = [
        pltpu.make_async_copy(q_hbm, q, in_sem.at[0]),
        pltpu.make_async_copy(k_hbm, k, in_sem.at[1]),
        pltpu.make_async_copy(v_hbm, v.at[:, pl.ds(0, HEAD)], in_sem.at[2]),
    ]
    w_loads = [
        pltpu.make_async_copy(w_hbm.at[:, block_cols(b, y)], w.at[3, b], in_sem.at[3 + b]) for b in range(2)
    ]
    for load in loads + w_loads:
        load.start()

    barrier = pltpu.get_barrier_semaphore()
    everyone = [d_kv, d_z, d_c, d_x, *d_y]
    for other in everyone:
        pl.semaphore_signal(barrier, 1, device_id=other, device_id_type=MESH)
    pl.semaphore_wait(barrier, len(everyone))

    kv = []
    for part in range(PARTS):
        rows = pl.ds(part * FAR, FAR)
        kv.append(
            (
                remote(k_hbm.at[rows], kf.at[rows], kv_ss.at[part, 0], kv_rs.at[part, 0], d_kv),
                remote(v_hbm.at[rows], vf.at[rows, pl.ds(0, HEAD)], kv_ss.at[part, 1], kv_rs.at[part, 1], d_kv),
            )
        )

    @pl.when(xl == 0)
    def _():
        for pair in kv:
            for copy in pair:
                copy.start()

    def quarter(zp, c):
        return pl.ds(pl.multiple_of((zp * 2 + c) * PIECE, PIECE), PIECE)

    mine, theirs = quarter(zp, c), quarter(1 - zp, c)
    wy = [
        [
            remote(w_hbm.at[mine, block_cols(b, ys[i])], w.at[i, b, mine], wy_ss.at[i, b], wy_rs.at[i, b], d_y[i])
            for b in range(2)
        ]
        for i in range(3)
    ]
    wz = [remote(w.at[i, :, mine], w.at[i, :, mine], wz_ss.at[i], wz_rs.at[i], d_z) for i in range(3)]
    wc = [
        [
            remote(w.at[i, :, rows], w.at[i, :, rows], wc_ss.at[j, i], wc_rs.at[j, i], d_c)
            for i in range(3)
        ]
        for j, rows in enumerate((mine, theirs))
    ]
    for pair in wy:
        for copy in pair:
            copy.start()

    def spread(i):
        for copy in wy[i]:
            copy.wait_recv()
        wz[i].start()
        wc[0][i].start()

    ones = jnp.ones((TOK, HEAD), BF16)
    v[:, pl.ds(HEAD, HEAD)] = ones
    vf[:, pl.ds(HEAD, HEAD)] = ones
    for load in loads:
        load.wait()

    def finish(rows, h, o, m):
        l = o[:, HEAD:]
        att[3, rows, pl.ds(h * HEAD, HEAD)] = (o[:, :HEAD] / l).astype(BF16)
        top[h, rows, :] = (m + jnp.log2(l)) * LN2

    def own(qi):
        rows = pl.ds(qi * QC, QC)
        causal = lax.broadcasted_iota(jnp.int32, (QC, QC), 0) >= lax.broadcasted_iota(jnp.int32, (QC, QC), 1)
        for h in range(GROUP):
            qh = q[rows, pl.ds(h * HEAD, HEAD)]
            sd = jnp.where(causal, dot_nt(qh, k[rows, :]) * SCALE, -1e30)
            m = jnp.max(sd, axis=1, keepdims=True)
            if qi:
                before = pl.ds(0, qi * QC)
                sb = dot_nt(qh, k[before, :]) * SCALE
                m = jnp.maximum(m, jnp.max(sb, axis=1, keepdims=True))
            o = dot_nn(jnp.exp2(sd - m).astype(BF16), v[rows, :])
            if qi:
                o += dot_nn(jnp.exp2(sb - m).astype(BF16), v[before, :])
            acc[h, rows, :] = o
            top[h, rows, :] = jnp.broadcast_to(m, (QC, HEAD))

    def far(part, qi):
        rows = pl.ds(pl.multiple_of(qi * QC, QC), QC)
        seen = pl.ds(part * FAR, FAR)
        for h in range(GROUP):
            sf = dot_nt(q[rows, pl.ds(h * HEAD, HEAD)], kf[seen, :]) * SCALE
            old = top[h, rows, :]
            m = jnp.maximum(old, jnp.broadcast_to(jnp.max(sf, axis=1, keepdims=True), (QC, HEAD)))
            keep = jnp.exp2(old - m)
            p = jnp.exp2(sf - jnp.concatenate([m] * (FAR // HEAD), axis=1))
            o = dot_nn(p.astype(BF16), vf[seen, :])
            o += acc[h, rows, :] * jnp.concatenate([keep, keep], axis=1)
            if part == PARTS - 1:
                finish(rows, h, o, m)
            else:
                acc[h, rows, :] = o
                top[h, rows, :] = m

    def step_rows(i):
        return pl.ds(pl.multiple_of(i * STEP, STEP), STEP)

    def direct(i, way):
        rows = step_rows(i)
        return remote(att.at[3, rows], att.at[way, rows], a_ss.at[way, i], a_rs.at[way, i], d_y[way])

    def forward(i, way):
        rows, cols = step_rows(i), pl.ds(way * HALF, HALF)
        return remote(
            att.at[way, rows, cols], att.at[2, rows, cols], f_ss.at[way, i], f_rs.at[way, i], d_y[way]
        )

    def send_direct(i):
        for way in range(2):
            direct(i, way).start()

    for qi in range(TOK // QC):
        own(qi)

    @pl.when(busy)
    def _():
        for part in range(PARTS - 1):
            for copy in kv[part]:
                copy.wait_recv()

            @pl.loop(0, TOK // QC)
            def _(qi):
                far(part, qi)

            if part == 1:
                spread(0)
                spread(1)

        for copy in kv[PARTS - 1]:
            copy.wait_recv()

        @pl.loop(0, TOK // QC)
        def _(qi):
            far(PARTS - 1, qi)

            @pl.when(qi == 0)
            def _():
                send_direct(0)
                send_direct(1)

    @pl.when(xl == 0)
    def _():
        @pl.loop(0, TOK // QC)
        def _(qi):
            rows = pl.ds(pl.multiple_of(qi * QC, QC), QC)
            for h in range(GROUP):
                finish(rows, h, acc[h, rows, :], top[h, rows, :])

            @pl.when(qi == 0)
            def _():
                send_direct(0)
                send_direct(1)

        spread(0)
        spread(1)

    spread(2)

    def pass_on(i):
        for way in range(2):
            direct(i, way).wait_recv()
            forward(i, way).start()

    def product(i, b):
        rows = step_rows(i)
        f = dot_nn(att[3, rows, :], w[3, b])
        for j in range(3):
            f += dot_nn(att[j, rows, :], w[j, b])
        return f

    def x_copy(i):
        rows = step_rows(i)
        return remote(xs.at[rows], xr.at[rows], x_ss.at[i], x_rs.at[i], d_x)

    def multiply(i):
        rows = step_rows(i)
        for way in range(2):
            forward(i, way).wait_recv()
        xs[rows, :] = product(i, 1).astype(BF16)
        x_copy(i).start()
        kept[rows, :] = product(i, 0)

    def collect(i):
        rows = step_rows(i)
        x_copy(i).wait_recv()
        out[rows, :] = (kept[rows, :] + xr[rows, :].astype(F32)).astype(BF16)

    pass_on(0)
    send_direct(2)
    pass_on(1)
    send_direct(3)

    for h in range(GROUP):
        for qi in range(TOK // QC):
            rows = pl.ds(qi * QC, QC)
            lse[pl.ds(h, 1), rows] = jnp.transpose(top[h, rows, :])[0:1, :]

    for i in range(3):
        wz[i].wait_recv()
        wc[1][i].start()
    for load in w_loads:
        load.wait()
    for j in range(2):
        for copy in wc[j]:
            copy.wait_recv()

    @pl.loop(2, NSTEP)
    def _(i):
        pass_on(i)

        @pl.when(i + 2 < NSTEP)
        def _():
            send_direct(i + 2)

        multiply(i - 2)

        @pl.when(i >= 4)
        def _():
            collect(i - 4)

    multiply(NSTEP - 2)
    multiply(NSTEP - 1)
    for i in range(NSTEP - 4, NSTEP):
        collect(i)

    @pl.when(xl == 0)
    def _():
        for pair in kv:
            for copy in pair:
                copy.wait_send()

    for copy in [*wy[0], *wy[1], *wy[2], *wz, *wc[0], *wc[1]]:
        copy.wait_send()

    @pl.loop(0, NSTEP)
    def _(i):
        for way in range(2):
            direct(i, way).wait_send()
            forward(i, way).wait_send()
        x_copy(i).wait_send()


def body(queries, keys, values, out_weight):
    dma = pltpu.SemaphoreType.DMA
    anywhere = pl.BlockSpec(memory_space=pl.ANY)
    return pl.pallas_call(
        kernel,
        out_shape=(
            jax.ShapeDtypeStruct((TOK, BLK), BF16),
            jax.ShapeDtypeStruct((GROUP, TOK), F32),
        ),
        in_specs=[anywhere] * 4,
        out_specs=(pl.BlockSpec(memory_space=pltpu.VMEM), pl.BlockSpec(memory_space=pltpu.VMEM)),
        scratch_shapes=[
            pltpu.VMEM((TOK, BLK), BF16),
            pltpu.VMEM((TOK, HEAD), BF16),
            pltpu.VMEM((TOK, 2 * HEAD), BF16),
            pltpu.VMEM((TOK, HEAD), BF16),
            pltpu.VMEM((TOK, 2 * HEAD), BF16),
            pltpu.VMEM((4, 2, BLK, BLK), BF16),
            pltpu.VMEM((4, TOK, BLK), BF16),
            pltpu.VMEM((GROUP, TOK, 2 * HEAD), F32),
            pltpu.VMEM((GROUP, TOK, HEAD), F32),
            pltpu.VMEM((TOK, BLK), F32),
            pltpu.VMEM((TOK, BLK), BF16),
            pltpu.VMEM((TOK, BLK), BF16),
            dma((5,)),
            dma((PARTS, 2)),
            dma((PARTS, 2)),
            dma((3, 2)),
            dma((3, 2)),
            dma((3,)),
            dma((3,)),
            dma((2, 3)),
            dma((2, 3)),
            dma((2, NSTEP)),
            dma((2, NSTEP)),
            dma((2, NSTEP)),
            dma((2, NSTEP)),
            dma((NSTEP,)),
            dma((NSTEP,)),
        ],
        compiler_params=pltpu.CompilerParams(
            collective_id=0, has_side_effects=True, vmem_limit_bytes=60 * 2**20
        ),
        cost_estimate=pl.CostEstimate(flops=10**10, bytes_accessed=8 * 2**20, transcendentals=8 * 2**20),
    )(queries, keys, values, out_weight)


def solution(mesh):
    in_specs = (P("seq", "kvh"), P("seq", "kvh"), P("seq", "kvh"), P("kvh", None))
    out_specs = (P("seq", "kvh"), P("kvh", "seq"))
    return jax.shard_map(body, mesh=mesh, in_specs=in_specs, out_specs=out_specs, check_vma=False)
```

```python
import functools
import math

import jax
import jax.numpy as jnp
from jax import lax
from jax.experimental import pallas as pl
from jax.experimental.pallas import tpu as pltpu
from jax.sharding import PartitionSpec as P

MESH = pl.DeviceIdType.MESH
HEAD = 128
GROUP = 4
TOK = 1024
QC = 256
FAR = 512
PARTS = TOK // FAR
STEP = 128
NSTEP = TOK // STEP
BLK = 512
HALF = STEP // 2
AHEAD = 3
LATE = NSTEP // 2
LAG = LATE + 1
WIDE = 4 * BLK
PIECE = 128
SCALE = math.log2(math.e) / math.sqrt(HEAD)
LN2 = math.log(2.0)
F32 = jnp.float32
BF16 = jnp.bfloat16


def dot_nt(a, b):
    return lax.dot_general(a, b, (((1,), (1,)), ((), ())), preferred_element_type=F32)


def dot_nn(a, b):
    return jnp.dot(a, b, preferred_element_type=F32)


def kernel(
    q_hbm, k_hbm, v_hbm, w_hbm, out, lse,
    q, k, v, kf, vf, w, att, acc, top, kept, xs, xr,
    in_sem, kv_ss, kv_rs, wy_ss, wy_rs, wz_ss, wz_rs, wc_ss, wc_rs, a_ss, a_rs, f_ss, f_rs, x_ss, x_rs,
):
    s = lax.axis_index("seq")
    g = lax.axis_index("kvh")
    xl, z, c = s // 16, (s // 2) % 8, s % 2
    xh, y = g // 4, g % 4
    busy = xl == 1

    def dev(xl=xl, z=z, c=c, xh=xh, y=y):
        return ((xl * 8 + z) * 2 + c, xh * 4 + y)

    zp = z % 2
    d_kv = dev(xl=1 - xl)
    d_z = dev(z=z + 1 - 2 * zp)
    d_c = dev(c=1 - c)
    d_x = dev(xh=1 - xh)
    ys = [(y + 1) % 4, (y + 3) % 4, (y + 2) % 4]
    d_y = [dev(y=other) for other in ys]

    def remote(src, dst, ss, rs, to):
        return pltpu.make_async_remote_copy(
            src_ref=src, dst_ref=dst, send_sem=ss, recv_sem=rs, device_id=to, device_id_type=MESH
        )

    def block_cols(b, owner):
        first = (xh if b == 0 else 1 - xh) * WIDE + owner * BLK
        return pl.ds(pl.multiple_of(first, BLK), BLK)

    loads = [
        pltpu.make_async_copy(q_hbm, q, in_sem.at[0]),
        pltpu.make_async_copy(k_hbm, k, in_sem.at[1]),
        pltpu.make_async_copy(v_hbm, v.at[:, pl.ds(0, HEAD)], in_sem.at[2]),
    ]
    w_loads = [
        pltpu.make_async_copy(w_hbm.at[:, block_cols(b, y)], w.at[3, b], in_sem.at[3 + b]) for b in range(2)
    ]
    for load in loads + w_loads:
        load.start()

    barrier = pltpu.get_barrier_semaphore()
    everyone = [d_kv, d_z, d_c, d_x, *d_y]
    for other in everyone:
        pl.semaphore_signal(barrier, 1, device_id=other, device_id_type=MESH)
    pl.semaphore_wait(barrier, len(everyone))

    kv = []
    for part in range(PARTS):
        rows = pl.ds(part * FAR, FAR)
        kv.append(
            (
                remote(k_hbm.at[rows], kf.at[rows], kv_ss.at[part, 0], kv_rs.at[part, 0], d_kv),
                remote(v_hbm.at[rows], vf.at[rows, pl.ds(0, HEAD)], kv_ss.at[part, 1], kv_rs.at[part, 1], d_kv),
            )
        )

    @pl.when(xl == 0)
    def _():
        for pair in kv:
            for copy in pair:
                copy.start()

    def quarter(zp, c):
        return pl.ds(pl.multiple_of((zp * 2 + c) * PIECE, PIECE), PIECE)

    mine, theirs = quarter(zp, c), quarter(1 - zp, c)
    wy = [
        [
            remote(w_hbm.at[mine, block_cols(b, ys[i])], w.at[i, b, mine], wy_ss.at[i, b], wy_rs.at[i, b], d_y[i])
            for b in range(2)
        ]
        for i in range(3)
    ]
    wz = [
        [remote(w.at[i, b, mine], w.at[i, b, mine], wz_ss.at[i, b], wz_rs.at[i, b], d_z) for b in range(2)]
        for i in range(3)
    ]
    wc = [
        [
            [remote(w.at[i, b, rows], w.at[i, b, rows], wc_ss.at[j, i, b], wc_rs.at[j, i, b], d_c) for b in range(2)]
            for i in range(3)
        ]
        for j, rows in enumerate((mine, theirs))
    ]
    for b in (1, 0):
        for i in range(3):
            wy[i][b].start()

    def spread(b):
        for i in range(3):
            wy[i][b].wait_recv()
            wz[i][b].start()
            wc[0][i][b].start()

    def gather(b):
        for i in range(3):
            wz[i][b].wait_recv()
            wc[1][i][b].start()

    def ready(b):
        w_loads[b].wait()
        for j in range(2):
            for i in range(3):
                wc[j][i][b].wait_recv()

    ones = jnp.ones((TOK, HEAD), BF16)
    v[:, pl.ds(HEAD, HEAD)] = ones
    vf[:, pl.ds(HEAD, HEAD)] = ones
    for load in loads:
        load.wait()

    def finish(rows, h, o, m):
        l = o[:, HEAD:]
        att[3, rows, pl.ds(h * HEAD, HEAD)] = (o[:, :HEAD] / l).astype(BF16)
        top[h, rows, :] = (m + jnp.log2(l)) * LN2

    def own(qi):
        rows = pl.ds(qi * QC, QC)
        causal = lax.broadcasted_iota(jnp.int32, (QC, QC), 0) >= lax.broadcasted_iota(jnp.int32, (QC, QC), 1)
        for h in range(GROUP):
            qh = q[rows, pl.ds(h * HEAD, HEAD)]
            sd = jnp.where(causal, dot_nt(qh, k[rows, :]) * SCALE, -1e30)
            m = jnp.max(sd, axis=1, keepdims=True)
            if qi:
                before = pl.ds(0, qi * QC)
                sb = dot_nt(qh, k[before, :]) * SCALE
                m = jnp.maximum(m, jnp.max(sb, axis=1, keepdims=True))
            o = dot_nn(jnp.exp2(sd - m).astype(BF16), v[rows, :])
            if qi:
                o += dot_nn(jnp.exp2(sb - m).astype(BF16), v[before, :])
            acc[h, rows, :] = o
            top[h, rows, :] = jnp.broadcast_to(m, (QC, HEAD))

    def far(part, qi):
        rows = pl.ds(pl.multiple_of(qi * QC, QC), QC)
        seen = pl.ds(part * FAR, FAR)
        for h in range(GROUP):
            sf = dot_nt(q[rows, pl.ds(h * HEAD, HEAD)], kf[seen, :]) * SCALE
            old = top[h, rows, :]
            m = jnp.maximum(old, jnp.broadcast_to(jnp.max(sf, axis=1, keepdims=True), (QC, HEAD)))
            keep = jnp.exp2(old - m)
            p = jnp.exp2(sf - jnp.concatenate([m] * (FAR // HEAD), axis=1))
            o = dot_nn(p.astype(BF16), vf[seen, :])
            o += acc[h, rows, :] * jnp.concatenate([keep, keep], axis=1)
            if part == PARTS - 1:
                finish(rows, h, o, m)
            else:
                acc[h, rows, :] = o
                top[h, rows, :] = m

    def step_rows(i):
        return pl.ds(pl.multiple_of(i * STEP, STEP), STEP)

    def direct(i, way):
        rows = step_rows(i)
        return remote(att.at[3, rows], att.at[way, rows], a_ss.at[way, i], a_rs.at[way, i], d_y[way])

    def forward(i, way):
        rows = pl.ds(pl.multiple_of(i * STEP + way * HALF, HALF), HALF)
        return remote(att.at[way, rows], att.at[2, rows], f_ss.at[way, i], f_rs.at[way, i], d_y[way])

    def send_direct(i):
        for way in range(2):
            direct(i, way).start()

    for qi in range(TOK // QC):
        own(qi)

    @pl.when(busy)
    def _():
        spread(1)
        for part in range(PARTS - 1):
            for copy in kv[part]:
                copy.wait_recv()

            @pl.loop(0, TOK // QC)
            def _(qi):
                far(part, qi)

        for copy in kv[PARTS - 1]:
            copy.wait_recv()

        @pl.loop(0, TOK // QC)
        def _(qi):
            far(PARTS - 1, qi)

            for i in range(AHEAD):

                @pl.when(qi == i * STEP // QC)
                def _():
                    send_direct(i)

    @pl.when(xl == 0)
    def _():
        @pl.loop(0, TOK // QC)
        def _(qi):
            rows = pl.ds(pl.multiple_of(qi * QC, QC), QC)
            for h in range(GROUP):
                finish(rows, h, acc[h, rows, :], top[h, rows, :])

            for i in range(AHEAD):

                @pl.when(qi == i * STEP // QC)
                def _():
                    send_direct(i)

        spread(1)

    spread(0)

    def pass_on(i):
        for way in range(2):
            direct(i, way).wait_recv()
            forward(i, way).start()

    def product(i, b):
        rows = step_rows(i)
        f = dot_nn(att[3, rows, :], w[3, b])
        for j in range(3):
            f += dot_nn(att[j, rows, :], w[j, b])
        return f

    def x_copy(i):
        rows = step_rows(i)
        return remote(xs.at[rows], xr.at[rows], x_ss.at[i], x_rs.at[i], d_x)

    def multiply_theirs(i):
        for way in range(2):
            forward(i, way).wait_recv()
        xs[step_rows(i), :] = product(i, 1).astype(BF16)
        x_copy(i).start()

    def multiply_mine(i):
        kept[step_rows(i), :] = product(i, 0)

    def collect(i):
        rows = step_rows(i)
        x_copy(i).wait_recv()
        out[rows, :] = (kept[rows, :] + xr[rows, :].astype(F32)).astype(BF16)

    for i in range(2):
        pass_on(i)
        send_direct(i + AHEAD)

    for h in range(GROUP):
        for qi in range(TOK // QC):
            rows = pl.ds(qi * QC, QC)
            lse[pl.ds(h, 1), rows] = jnp.transpose(top[h, rows, :])[0:1, :]

    gather(1)
    ready(1)

    @pl.loop(2, NSTEP)
    def _(i):
        pass_on(i)

        @pl.when(i + AHEAD < NSTEP)
        def _():
            send_direct(i + AHEAD)

        multiply_theirs(i - 2)

        @pl.when(i == LATE - 1)
        def _():
            gather(0)

        @pl.when(i == LATE)
        def _():
            ready(0)

        @pl.when(i >= LATE)
        def _():
            for j in range(2):
                at = 2 * (i - LATE) + j

                @pl.when(at <= i - 2)
                def _():
                    multiply_mine(at)

        @pl.when(i >= LAG)
        def _():
            collect(i - LAG)

    multiply_theirs(NSTEP - 2)
    multiply_mine(NSTEP - 3)
    for i in range(NSTEP - LAG, NSTEP - 3):
        collect(i)
    multiply_theirs(NSTEP - 1)
    multiply_mine(NSTEP - 2)
    multiply_mine(NSTEP - 1)
    for i in range(NSTEP - 3, NSTEP):
        collect(i)

    @pl.when(xl == 0)
    def _():
        for pair in kv:
            for copy in pair:
                copy.wait_send()

    for i in range(3):
        for b in range(2):
            for copy in (wy[i][b], wz[i][b], wc[0][i][b], wc[1][i][b]):
                copy.wait_send()

    @pl.loop(0, NSTEP)
    def _(i):
        for way in range(2):
            direct(i, way).wait_send()
            forward(i, way).wait_send()
        x_copy(i).wait_send()


def body(queries, keys, values, out_weight):
    dma = pltpu.SemaphoreType.DMA
    anywhere = pl.BlockSpec(memory_space=pl.ANY)
    return pl.pallas_call(
        kernel,
        out_shape=(
            pltpu.VMEM((TOK, BLK), BF16),
            pltpu.VMEM((GROUP, TOK), F32),
        ),
        in_specs=[anywhere] * 4,
        out_specs=(pl.BlockSpec(memory_space=pltpu.VMEM), pl.BlockSpec(memory_space=pltpu.VMEM)),
        scratch_shapes=[
            pltpu.VMEM((TOK, BLK), BF16),
            pltpu.VMEM((TOK, HEAD), BF16),
            pltpu.VMEM((TOK, 2 * HEAD), BF16),
            pltpu.VMEM((TOK, HEAD), BF16),
            pltpu.VMEM((TOK, 2 * HEAD), BF16),
            pltpu.VMEM((4, 2, BLK, BLK), BF16),
            pltpu.VMEM((4, TOK, BLK), BF16),
            pltpu.VMEM((GROUP, TOK, 2 * HEAD), F32),
            pltpu.VMEM((GROUP, TOK, HEAD), F32),
            pltpu.VMEM((TOK, BLK), F32),
            pltpu.VMEM((TOK, BLK), BF16),
            pltpu.VMEM((TOK, BLK), BF16),
            dma((5,)),
            dma((PARTS, 2)),
            dma((PARTS, 2)),
            dma((3, 2)),
            dma((3, 2)),
            dma((3, 2)),
            dma((3, 2)),
            dma((2, 3, 2)),
            dma((2, 3, 2)),
            dma((2, NSTEP)),
            dma((2, NSTEP)),
            dma((2, NSTEP)),
            dma((2, NSTEP)),
            dma((NSTEP,)),
            dma((NSTEP,)),
        ],
        compiler_params=pltpu.CompilerParams(
            collective_id=0, has_side_effects=True, vmem_limit_bytes=60 * 2**20
        ),
        cost_estimate=pl.CostEstimate(flops=10**10, bytes_accessed=8 * 2**20, transcendentals=8 * 2**20),
    )(queries, keys, values, out_weight)


def solution(mesh):
    in_specs = (P("seq", "kvh"), P("seq", "kvh"), P("seq", "kvh"), P("kvh", None))
    out_specs = (P("seq", "kvh"), P("kvh", "seq"))
    return jax.shard_map(body, mesh=mesh, in_specs=in_specs, out_specs=out_specs, check_vma=False)
```

```python
import functools
import math

import jax
import jax.numpy as jnp
from jax import lax
from jax.experimental import pallas as pl
from jax.experimental.pallas import tpu as pltpu
from jax.sharding import PartitionSpec as P

MESH = pl.DeviceIdType.MESH
HEAD = 128
GROUP = 4
TOK = 1024
QC = 256
FAR = 512
PARTS = TOK // FAR
STEP = 128
BLK = 512
FULL = 7
TAIL = 64
NCHUNK = FULL + (TOK - FULL * STEP) // TAIL
AHEAD = 3
LATE = 4
LAG = LATE + 1
WIDE = 4 * BLK
PIECE = 128
SCALE = math.log2(math.e) / math.sqrt(HEAD)
LN2 = math.log(2.0)
F32 = jnp.float32
BF16 = jnp.bfloat16


def dot_nt(a, b):
    return lax.dot_general(a, b, (((1,), (1,)), ((), ())), preferred_element_type=F32)


def dot_nn(a, b):
    return jnp.dot(a, b, preferred_element_type=F32)


def kernel(
    q_hbm, k_hbm, v_hbm, w_hbm, out, lse,
    q, k, v, kf, vf, w, att, acc, top, kept, xs, xr,
    in_sem, kv_ss, kv_rs, wy_ss, wy_rs, wx_ss, wx_rs, wz_ss, wz_rs, wc_ss, wc_rs, a_ss, a_rs, f_ss, f_rs, x_ss, x_rs,
):
    s = lax.axis_index("seq")
    g = lax.axis_index("kvh")
    xl, z, c = s // 16, (s // 2) % 8, s % 2
    xh, y = g // 4, g % 4
    busy = xl == 1

    def dev(xl=xl, z=z, c=c, xh=xh, y=y):
        return ((xl * 8 + z) * 2 + c, xh * 4 + y)

    zp = z % 2
    d_kv = dev(xl=1 - xl)
    d_z = dev(z=z + 1 - 2 * zp)
    d_c = dev(c=1 - c)
    d_x = dev(xh=1 - xh)
    ys = [(y + 1) % 4, (y + 3) % 4, (y + 2) % 4]
    d_y = [dev(y=other) for other in ys]

    def remote(src, dst, ss, rs, to):
        return pltpu.make_async_remote_copy(
            src_ref=src, dst_ref=dst, send_sem=ss, recv_sem=rs, device_id=to, device_id_type=MESH
        )

    def block_cols(b, owner):
        first = (xh if b == 0 else 1 - xh) * WIDE + owner * BLK
        return pl.ds(pl.multiple_of(first, BLK), BLK)

    loads = [
        pltpu.make_async_copy(q_hbm, q, in_sem.at[0]),
        pltpu.make_async_copy(k_hbm, k, in_sem.at[1]),
        pltpu.make_async_copy(v_hbm, v.at[:, pl.ds(0, HEAD)], in_sem.at[2]),
    ]
    w_loads = [
        pltpu.make_async_copy(w_hbm.at[:, block_cols(b, y)], w.at[3, b], in_sem.at[3 + b]) for b in range(2)
    ]
    for load in loads + w_loads:
        load.start()

    barrier = pltpu.get_barrier_semaphore()
    everyone = [d_kv, d_z, d_c, d_x, *d_y]
    for other in everyone:
        pl.semaphore_signal(barrier, 1, device_id=other, device_id_type=MESH)
    pl.semaphore_wait(barrier, len(everyone))

    kv = []
    for part in range(PARTS):
        rows = pl.ds(part * FAR, FAR)
        kv.append(
            (
                remote(k_hbm.at[rows], kf.at[rows], kv_ss.at[part, 0], kv_rs.at[part, 0], d_kv),
                remote(v_hbm.at[rows], vf.at[rows, pl.ds(0, HEAD)], kv_ss.at[part, 1], kv_rs.at[part, 1], d_kv),
            )
        )

    @pl.when(xl == 0)
    def _():
        for pair in kv:
            for copy in pair:
                copy.start()

    def quarter(zp, c):
        return pl.ds(pl.multiple_of((zp * 2 + c) * PIECE, PIECE), PIECE)

    mine, theirs = quarter(zp, c), quarter(1 - zp, c)
    wy = [
        [
            remote(w_hbm.at[mine, block_cols(b, ys[i])], w.at[i, b, mine], wy_ss.at[i, b], wy_rs.at[i, b], d_y[i])
            for b in range(2)
        ]
        for i in range(3)
    ]
    wz = [
        [remote(w.at[i, b, mine], w.at[i, b, mine], wz_ss.at[i, b], wz_rs.at[i, b], d_z) for b in range(2)]
        for i in range(3)
    ]
    wc = [
        [
            [remote(w.at[i, b, rows], w.at[i, b, rows], wc_ss.at[j, i, b], wc_rs.at[j, i, b], d_c) for b in range(2)]
            for i in range(3)
        ]
        for j, rows in enumerate((mine, theirs))
    ]
    wx = [remote(w.at[i, 0, mine], w.at[i, 0, mine], wx_ss.at[i], wx_rs.at[i], d_kv) for i in range(3)]
    for i in range(3):
        wy[i][1].start()

    @pl.when(busy)
    def _():
        for i in range(3):
            wy[i][0].start()

    def spread(b, source=None):
        for i in range(3):
            (wy[i][b] if source is None else source[i]).wait_recv()
            wz[i][b].start()
            wc[0][i][b].start()

    def gather(b):
        for i in range(3):
            wz[i][b].wait_recv()
            wc[1][i][b].start()

    def ready(b):
        w_loads[b].wait()
        for j in range(2):
            for i in range(3):
                wc[j][i][b].wait_recv()

    ones = jnp.ones((TOK, HEAD), BF16)
    v[:, pl.ds(HEAD, HEAD)] = ones
    vf[:, pl.ds(HEAD, HEAD)] = ones
    for load in loads:
        load.wait()

    def finish(rows, h, o, m):
        l = o[:, HEAD:]
        att[3, rows, pl.ds(h * HEAD, HEAD)] = (o[:, :HEAD] / l).astype(BF16)
        top[h, rows, :] = (m + jnp.log2(l)) * LN2

    def own(qi):
        rows = pl.ds(qi * QC, QC)
        causal = lax.broadcasted_iota(jnp.int32, (QC, QC), 0) >= lax.broadcasted_iota(jnp.int32, (QC, QC), 1)
        for h in range(GROUP):
            qh = q[rows, pl.ds(h * HEAD, HEAD)]
            sd = jnp.where(causal, dot_nt(qh, k[rows, :]) * SCALE, -1e30)
            m = jnp.max(sd, axis=1, keepdims=True)
            if qi:
                before = pl.ds(0, qi * QC)
                sb = dot_nt(qh, k[before, :]) * SCALE
                m = jnp.maximum(m, jnp.max(sb, axis=1, keepdims=True))
            o = dot_nn(jnp.exp2(sd - m).astype(BF16), v[rows, :])
            if qi:
                o += dot_nn(jnp.exp2(sb - m).astype(BF16), v[before, :])
            acc[h, rows, :] = o
            top[h, rows, :] = jnp.broadcast_to(m, (QC, HEAD))

    def far(part, qi):
        rows = pl.ds(pl.multiple_of(qi * QC, QC), QC)
        seen = pl.ds(part * FAR, FAR)
        for h in range(GROUP):
            sf = dot_nt(q[rows, pl.ds(h * HEAD, HEAD)], kf[seen, :]) * SCALE
            old = top[h, rows, :]
            m = jnp.maximum(old, jnp.broadcast_to(jnp.max(sf, axis=1, keepdims=True), (QC, HEAD)))
            keep = jnp.exp2(old - m)
            p = jnp.exp2(sf - jnp.concatenate([m] * (FAR // HEAD), axis=1))
            o = dot_nn(p.astype(BF16), vf[seen, :])
            o += acc[h, rows, :] * jnp.concatenate([keep, keep], axis=1)
            if part == PARTS - 1:
                finish(rows, h, o, m)
            else:
                acc[h, rows, :] = o
                top[h, rows, :] = m

    def step_rows(i, part=None):
        if isinstance(i, int) and i >= FULL:
            first, size = FULL * STEP + (i - FULL) * TAIL, TAIL
        else:
            first, size = i * STEP, STEP
        if part is not None:
            first, size = first + part * (size // 2), size // 2
        return pl.ds(first if isinstance(first, int) else pl.multiple_of(first, size), size)

    def direct(i, way):
        rows = step_rows(i)
        return remote(att.at[3, rows], att.at[way, rows], a_ss.at[way, i], a_rs.at[way, i], d_y[way])

    def forward(i, way):
        rows = step_rows(i, way)
        return remote(att.at[way, rows], att.at[2, rows], f_ss.at[way, i], f_rs.at[way, i], d_y[way])

    def send_direct(i):
        for way in range(2):
            direct(i, way).start()

    for qi in range(TOK // QC):
        own(qi)

    @pl.when(busy)
    def _():
        spread(1)
        for part in range(PARTS - 1):
            for copy in kv[part]:
                copy.wait_recv()

            @pl.loop(0, TOK // QC)
            def _(qi):
                far(part, qi)

        for copy in kv[PARTS - 1]:
            copy.wait_recv()

        @pl.loop(0, TOK // QC)
        def _(qi):
            far(PARTS - 1, qi)

            for i in range(AHEAD):

                @pl.when(qi == i * STEP // QC)
                def _():
                    send_direct(i)

    @pl.when(xl == 0)
    def _():
        @pl.loop(0, TOK // QC)
        def _(qi):
            rows = pl.ds(pl.multiple_of(qi * QC, QC), QC)
            for h in range(GROUP):
                finish(rows, h, acc[h, rows, :], top[h, rows, :])

            for i in range(AHEAD):

                @pl.when(qi == i * STEP // QC)
                def _():
                    send_direct(i)

        spread(1)

    @pl.when(busy)
    def _():
        spread(0)
        for copy in wx:
            copy.start()

    def pass_on(i):
        for way in range(2):
            direct(i, way).wait_recv()
            forward(i, way).start()

    def product(i, b):
        rows = step_rows(i)
        f = dot_nn(att[3, rows, :], w[3, b])
        for j in range(3):
            f += dot_nn(att[j, rows, :], w[j, b])
        return f

    def x_copy(i):
        rows = step_rows(i)
        return remote(xs.at[rows], xr.at[rows], x_ss.at[i], x_rs.at[i], d_x)

    def multiply_theirs(i):
        for way in range(2):
            forward(i, way).wait_recv()
        xs[step_rows(i), :] = product(i, 1).astype(BF16)
        x_copy(i).start()

    def multiply_mine(i):
        kept[step_rows(i), :] = product(i, 0)

    def collect(i):
        rows = step_rows(i)
        x_copy(i).wait_recv()
        out[rows, :] = (kept[rows, :] + xr[rows, :].astype(F32)).astype(BF16)

    for i in range(2):
        pass_on(i)
        send_direct(i + AHEAD)

    for h in range(GROUP):
        for qi in range(TOK // QC):
            rows = pl.ds(qi * QC, QC)
            lse[pl.ds(h, 1), rows] = jnp.transpose(top[h, rows, :])[0:1, :]

    gather(1)
    ready(1)

    @pl.loop(2, FULL)
    def _(i):
        pass_on(i)

        @pl.when(i + AHEAD < FULL)
        def _():
            send_direct(i + AHEAD)

        for chunk in range(FULL, NCHUNK):

            @pl.when(i + AHEAD == chunk)
            def _():
                send_direct(chunk)

        multiply_theirs(i - 2)

        @pl.when((i == LATE) & (xl == 0))
        def _():
            spread(0, wx)

        @pl.when(i == LATE + 2 - 3 * xl)
        def _():
            gather(0)

        @pl.when((i == LATE) & busy)
        def _():
            ready(0)

        @pl.when((i >= LATE) & busy)
        def _():
            for j in range(2):
                at = 2 * (i - LATE) + j

                @pl.when(at <= i - 2)
                def _():
                    multiply_mine(at)

        @pl.when((i >= LAG) & busy)
        def _():
            collect(i - LAG)

    pass_on(7)
    multiply_theirs(5)

    @pl.when(xl == 0)
    def _():
        ready(0)

        @pl.loop(0, LATE + 1)
        def _(i):
            multiply_mine(i)

    multiply_mine(5)
    collect(2)
    pass_on(8)
    multiply_theirs(6)

    @pl.when(xl == 0)
    def _():
        collect(0)
        collect(1)

    multiply_theirs(7)
    multiply_mine(6)
    collect(3)
    collect(4)
    multiply_theirs(8)
    multiply_mine(7)
    multiply_mine(8)
    for i in range(5, NCHUNK):
        collect(i)

    @pl.when(xl == 0)
    def _():
        for pair in kv:
            for copy in pair:
                copy.wait_send()

    for i in range(3):
        for b in range(2):
            for copy in (wz[i][b], wc[0][i][b], wc[1][i][b]):
                copy.wait_send()
        wy[i][1].wait_send()

        @pl.when(busy)
        def _():
            wy[i][0].wait_send()
            wx[i].wait_send()

    def sent(i):
        for way in range(2):
            direct(i, way).wait_send()
            forward(i, way).wait_send()
        x_copy(i).wait_send()

    pl.loop(0, FULL)(sent)
    for i in range(FULL, NCHUNK):
        sent(i)


def body(queries, keys, values, out_weight):
    dma = pltpu.SemaphoreType.DMA
    anywhere = pl.BlockSpec(memory_space=pl.ANY)
    return pl.pallas_call(
        kernel,
        out_shape=(
            pltpu.VMEM((TOK, BLK), BF16),
            pltpu.VMEM((GROUP, TOK), F32),
        ),
        in_specs=[anywhere] * 4,
        out_specs=(pl.BlockSpec(memory_space=pltpu.VMEM), pl.BlockSpec(memory_space=pltpu.VMEM)),
        scratch_shapes=[
            pltpu.VMEM((TOK, BLK), BF16),
            pltpu.VMEM((TOK, HEAD), BF16),
            pltpu.VMEM((TOK, 2 * HEAD), BF16),
            pltpu.VMEM((TOK, HEAD), BF16),
            pltpu.VMEM((TOK, 2 * HEAD), BF16),
            pltpu.VMEM((4, 2, BLK, BLK), BF16),
            pltpu.VMEM((4, TOK, BLK), BF16),
            pltpu.VMEM((GROUP, TOK, 2 * HEAD), F32),
            pltpu.VMEM((GROUP, TOK, HEAD), F32),
            pltpu.VMEM((TOK, BLK), F32),
            pltpu.VMEM((TOK, BLK), BF16),
            pltpu.VMEM((TOK, BLK), BF16),
            dma((5,)),
            dma((PARTS, 2)),
            dma((PARTS, 2)),
            dma((3, 2)),
            dma((3, 2)),
            dma((3,)),
            dma((3,)),
            dma((3, 2)),
            dma((3, 2)),
            dma((2, 3, 2)),
            dma((2, 3, 2)),
            dma((2, NCHUNK)),
            dma((2, NCHUNK)),
            dma((2, NCHUNK)),
            dma((2, NCHUNK)),
            dma((NCHUNK,)),
            dma((NCHUNK,)),
        ],
        compiler_params=pltpu.CompilerParams(
            collective_id=0, has_side_effects=True, vmem_limit_bytes=60 * 2**20
        ),
        cost_estimate=pl.CostEstimate(flops=10**10, bytes_accessed=8 * 2**20, transcendentals=8 * 2**20),
    )(queries, keys, values, out_weight)


def solution(mesh):
    in_specs = (P("seq", "kvh"), P("seq", "kvh"), P("seq", "kvh"), P("kvh", None))
    out_specs = (P("seq", "kvh"), P("kvh", "seq"))
    return jax.shard_map(body, mesh=mesh, in_specs=in_specs, out_specs=out_specs, check_vma=False)
```

```python
import functools
import math

import jax
import jax.numpy as jnp
from jax import lax
from jax.experimental import pallas as pl
from jax.experimental.pallas import tpu as pltpu
from jax.sharding import PartitionSpec as P

MESH = pl.DeviceIdType.MESH
HEAD = 128
GROUP = 4
TOK = 1024
QC = 128
FAR = 512
PARTS = TOK // FAR
STEP = 128
BLK = 512
FULL = 7
TAIL = 64
NCHUNK = FULL + (TOK - FULL * STEP) // TAIL
AHEAD = 3
LATE = 4
LAG = LATE + 1
WIDE = 4 * BLK
PIECE = 128
SCALE = math.log2(math.e) / math.sqrt(HEAD)
LN2 = math.log(2.0)
F32 = jnp.float32
BF16 = jnp.bfloat16


def dot_nt(a, b):
    return lax.dot_general(a, b, (((1,), (1,)), ((), ())), preferred_element_type=F32)


def dot_nn(a, b):
    return jnp.dot(a, b, preferred_element_type=F32)


def kernel(
    q_hbm, k_hbm, v_hbm, w_hbm, out, lse,
    q, k, v, kf, vf, w, att, acc, top, kept, xs, xr,
    in_sem, kv_ss, kv_rs, wy_ss, wy_rs, wx_ss, wx_rs, wz_ss, wz_rs, wc_ss, wc_rs, a_ss, a_rs, f_ss, f_rs, x_ss, x_rs,
):
    s = lax.axis_index("seq")
    g = lax.axis_index("kvh")
    xl, z, c = s // 16, (s // 2) % 8, s % 2
    xh, y = g // 4, g % 4
    busy = xl == 1

    def dev(xl=xl, z=z, c=c, xh=xh, y=y):
        return ((xl * 8 + z) * 2 + c, xh * 4 + y)

    zp = z % 2
    d_kv = dev(xl=1 - xl)
    d_z = dev(z=z + 1 - 2 * zp)
    d_c = dev(c=1 - c)
    d_x = dev(xh=1 - xh)
    ys = [(y + 1) % 4, (y + 3) % 4, (y + 2) % 4]
    d_y = [dev(y=other) for other in ys]

    def remote(src, dst, ss, rs, to):
        return pltpu.make_async_remote_copy(
            src_ref=src, dst_ref=dst, send_sem=ss, recv_sem=rs, device_id=to, device_id_type=MESH
        )

    def block_cols(b, owner):
        first = (xh if b == 0 else 1 - xh) * WIDE + owner * BLK
        return pl.ds(pl.multiple_of(first, BLK), BLK)

    loads = [
        pltpu.make_async_copy(q_hbm, q, in_sem.at[0]),
        pltpu.make_async_copy(k_hbm, k, in_sem.at[1]),
        pltpu.make_async_copy(v_hbm, v.at[:, pl.ds(0, HEAD)], in_sem.at[2]),
    ]
    w_loads = [
        pltpu.make_async_copy(w_hbm.at[:, block_cols(b, y)], w.at[3, b], in_sem.at[3 + b]) for b in range(2)
    ]
    for load in loads + w_loads:
        load.start()

    barrier = pltpu.get_barrier_semaphore()
    everyone = [d_kv, d_z, d_c, d_x, *d_y]
    for other in everyone:
        pl.semaphore_signal(barrier, 1, device_id=other, device_id_type=MESH)
    pl.semaphore_wait(barrier, len(everyone))

    kv = []
    for part in range(PARTS):
        rows = pl.ds(part * FAR, FAR)
        kv.append(
            (
                remote(k_hbm.at[rows], kf.at[rows], kv_ss.at[part, 0], kv_rs.at[part, 0], d_kv),
                remote(v_hbm.at[rows], vf.at[rows, pl.ds(0, HEAD)], kv_ss.at[part, 1], kv_rs.at[part, 1], d_kv),
            )
        )

    @pl.when(xl == 0)
    def _():
        for pair in kv:
            for copy in pair:
                copy.start()

    def quarter(zp, c):
        return pl.ds(pl.multiple_of((zp * 2 + c) * PIECE, PIECE), PIECE)

    mine, theirs = quarter(zp, c), quarter(1 - zp, c)
    wy = [
        [
            remote(w_hbm.at[mine, block_cols(b, ys[i])], w.at[i, b, mine], wy_ss.at[i, b], wy_rs.at[i, b], d_y[i])
            for b in range(2)
        ]
        for i in range(3)
    ]
    wz = [
        [remote(w.at[i, b, mine], w.at[i, b, mine], wz_ss.at[i, b], wz_rs.at[i, b], d_z) for b in range(2)]
        for i in range(3)
    ]
    wc = [
        [
            [remote(w.at[i, b, rows], w.at[i, b, rows], wc_ss.at[j, i, b], wc_rs.at[j, i, b], d_c) for b in range(2)]
            for i in range(3)
        ]
        for j, rows in enumerate((mine, theirs))
    ]
    wx = [remote(w.at[i, 0, mine], w.at[i, 0, mine], wx_ss.at[i], wx_rs.at[i], d_kv) for i in range(3)]
    for i in range(3):
        wy[i][1].start()

    @pl.when(busy)
    def _():
        for i in range(3):
            wy[i][0].start()

    def spread(b, source=None):
        for i in range(3):
            (wy[i][b] if source is None else source[i]).wait_recv()
            wz[i][b].start()
            wc[0][i][b].start()

    def gather(b):
        for i in range(3):
            wz[i][b].wait_recv()
            wc[1][i][b].start()

    def ready(b):
        w_loads[b].wait()
        for j in range(2):
            for i in range(3):
                wc[j][i][b].wait_recv()

    ones = jnp.ones((TOK, HEAD), BF16)
    v[:, pl.ds(HEAD, HEAD)] = ones
    vf[:, pl.ds(HEAD, HEAD)] = ones
    for load in loads:
        load.wait()

    def finish(rows, h, o, m):
        l = o[:, HEAD:]
        att[3, rows, pl.ds(h * HEAD, HEAD)] = (o[:, :HEAD] / l).astype(BF16)
        top[h, rows, :] = (m + jnp.log2(l)) * LN2

    def own(qi):
        rows = pl.ds(qi * QC, QC)
        causal = lax.broadcasted_iota(jnp.int32, (QC, QC), 0) >= lax.broadcasted_iota(jnp.int32, (QC, QC), 1)
        for h in range(GROUP):
            qh = q[rows, pl.ds(h * HEAD, HEAD)]
            sd = jnp.where(causal, dot_nt(qh, k[rows, :]) * SCALE, -1e30)
            m = jnp.max(sd, axis=1, keepdims=True)
            if qi:
                before = pl.ds(0, qi * QC)
                sb = dot_nt(qh, k[before, :]) * SCALE
                m = jnp.maximum(m, jnp.max(sb, axis=1, keepdims=True))
            o = dot_nn(jnp.exp2(sd - m).astype(BF16), v[rows, :])
            if qi:
                o += dot_nn(jnp.exp2(sb - m).astype(BF16), v[before, :])
            acc[h, rows, :] = o
            top[h, rows, :] = jnp.broadcast_to(m, (QC, HEAD))

    def far(part, qi):
        rows = pl.ds(pl.multiple_of(qi * QC, QC), QC)
        seen = pl.ds(part * FAR, FAR)
        for h in range(GROUP):
            sf = dot_nt(q[rows, pl.ds(h * HEAD, HEAD)], kf[seen, :]) * SCALE
            old = top[h, rows, :]
            m = jnp.maximum(old, jnp.broadcast_to(jnp.max(sf, axis=1, keepdims=True), (QC, HEAD)))
            keep = jnp.exp2(old - m)
            p = jnp.exp2(sf - jnp.concatenate([m] * (FAR // HEAD), axis=1))
            o = dot_nn(p.astype(BF16), vf[seen, :])
            o += acc[h, rows, :] * jnp.concatenate([keep, keep], axis=1)
            if part == PARTS - 1:
                finish(rows, h, o, m)
            else:
                acc[h, rows, :] = o
                top[h, rows, :] = m

    def step_rows(i, part=None):
        if isinstance(i, int) and i >= FULL:
            first, size = FULL * STEP + (i - FULL) * TAIL, TAIL
        else:
            first, size = i * STEP, STEP
        if part is not None:
            first, size = first + part * (size // 2), size // 2
        return pl.ds(first if isinstance(first, int) else pl.multiple_of(first, size), size)

    def direct(i, way):
        rows = step_rows(i)
        return remote(att.at[3, rows], att.at[way, rows], a_ss.at[way, i], a_rs.at[way, i], d_y[way])

    def forward(i, way):
        rows = step_rows(i, way)
        return remote(att.at[way, rows], att.at[2, rows], f_ss.at[way, i], f_rs.at[way, i], d_y[way])

    def send_direct(i):
        for way in range(2):
            direct(i, way).start()

    for qi in range(TOK // QC):
        own(qi)

    @pl.when(busy)
    def _():
        for part in range(PARTS - 1):
            for copy in kv[part]:
                copy.wait_recv()

            @pl.loop(0, TOK // QC)
            def _(qi):
                far(part, qi)

        spread(1)
        for copy in kv[PARTS - 1]:
            copy.wait_recv()

        @pl.loop(0, TOK // QC)
        def _(qi):
            far(PARTS - 1, qi)

            for i in range(AHEAD):

                @pl.when(qi == i * STEP // QC)
                def _():
                    send_direct(i)

    @pl.when(xl == 0)
    def _():
        @pl.loop(0, TOK // QC)
        def _(qi):
            rows = pl.ds(pl.multiple_of(qi * QC, QC), QC)
            for h in range(GROUP):
                finish(rows, h, acc[h, rows, :], top[h, rows, :])

            for i in range(AHEAD):

                @pl.when(qi == i * STEP // QC)
                def _():
                    send_direct(i)

        spread(1)

    @pl.when(busy)
    def _():
        spread(0)
        for copy in wx:
            copy.start()

    def pass_on(i):
        for way in range(2):
            direct(i, way).wait_recv()
            forward(i, way).start()

    def product(i, b):
        rows = step_rows(i)
        f = dot_nn(att[3, rows, :], w[3, b])
        for j in range(3):
            f += dot_nn(att[j, rows, :], w[j, b])
        return f

    def x_copy(i):
        rows = step_rows(i)
        return remote(xs.at[rows], xr.at[rows], x_ss.at[i], x_rs.at[i], d_x)

    def multiply_theirs(i):
        for way in range(2):
            forward(i, way).wait_recv()
        xs[step_rows(i), :] = product(i, 1).astype(BF16)
        x_copy(i).start()

    def multiply_mine(i):
        kept[step_rows(i), :] = product(i, 0)

    def collect(i):
        rows = step_rows(i)
        x_copy(i).wait_recv()
        out[rows, :] = (kept[rows, :] + xr[rows, :].astype(F32)).astype(BF16)

    for i in range(2):
        pass_on(i)
        send_direct(i + AHEAD)

    for h in range(GROUP):
        for qi in range(TOK // QC):
            rows = pl.ds(qi * QC, QC)
            lse[pl.ds(h, 1), rows] = jnp.transpose(top[h, rows, :])[0:1, :]

    gather(1)
    ready(1)

    @pl.loop(2, FULL)
    def _(i):
        pass_on(i)

        @pl.when(i + AHEAD < FULL)
        def _():
            send_direct(i + AHEAD)

        for chunk in range(FULL, NCHUNK):

            @pl.when(i + AHEAD - 1 == chunk)
            def _():
                send_direct(chunk)

        multiply_theirs(i - 2)

        @pl.when((i == LATE) & (xl == 0))
        def _():
            spread(0, wx)

        @pl.when(i == LATE + 2 - 3 * xl)
        def _():
            gather(0)

        @pl.when((i == LATE) & busy)
        def _():
            ready(0)

        @pl.when((i >= LATE) & busy)
        def _():
            for j in range(2):
                at = 2 * (i - LATE) + j

                @pl.when(at <= i - 2)
                def _():
                    multiply_mine(at)

        @pl.when((i >= LAG) & busy)
        def _():
            collect(i - LAG)

    pass_on(7)
    multiply_theirs(5)
    multiply_theirs(6)
    pass_on(8)

    @pl.when(xl == 0)
    def _():
        ready(0)

        @pl.loop(0, LATE + 1)
        def _(i):
            multiply_mine(i)

        collect(0)
        collect(1)

    multiply_mine(5)
    multiply_theirs(7)
    collect(2)
    multiply_theirs(8)
    collect(3)
    for i in range(6, NCHUNK):
        multiply_mine(i)
    for i in range(4, NCHUNK):
        collect(i)

    @pl.when(xl == 0)
    def _():
        for pair in kv:
            for copy in pair:
                copy.wait_send()

    for i in range(3):
        for b in range(2):
            for copy in (wz[i][b], wc[0][i][b], wc[1][i][b]):
                copy.wait_send()
        wy[i][1].wait_send()

        @pl.when(busy)
        def _():
            wy[i][0].wait_send()
            wx[i].wait_send()

    def sent(i):
        for way in range(2):
            direct(i, way).wait_send()
            forward(i, way).wait_send()
        x_copy(i).wait_send()

    pl.loop(0, FULL)(sent)
    for i in range(FULL, NCHUNK):
        sent(i)


def body(queries, keys, values, out_weight):
    dma = pltpu.SemaphoreType.DMA
    anywhere = pl.BlockSpec(memory_space=pl.ANY)
    return pl.pallas_call(
        kernel,
        out_shape=(
            pltpu.VMEM((TOK, BLK), BF16),
            pltpu.VMEM((GROUP, TOK), F32),
        ),
        in_specs=[anywhere] * 4,
        out_specs=(pl.BlockSpec(memory_space=pltpu.VMEM), pl.BlockSpec(memory_space=pltpu.VMEM)),
        scratch_shapes=[
            pltpu.VMEM((TOK, BLK), BF16),
            pltpu.VMEM((TOK, HEAD), BF16),
            pltpu.VMEM((TOK, 2 * HEAD), BF16),
            pltpu.VMEM((TOK, HEAD), BF16),
            pltpu.VMEM((TOK, 2 * HEAD), BF16),
            pltpu.VMEM((4, 2, BLK, BLK), BF16),
            pltpu.VMEM((4, TOK, BLK), BF16),
            pltpu.VMEM((GROUP, TOK, 2 * HEAD), F32),
            pltpu.VMEM((GROUP, TOK, HEAD), F32),
            pltpu.VMEM((TOK, BLK), F32),
            pltpu.VMEM((TOK, BLK), BF16),
            pltpu.VMEM((TOK, BLK), BF16),
            dma((5,)),
            dma((PARTS, 2)),
            dma((PARTS, 2)),
            dma((3, 2)),
            dma((3, 2)),
            dma((3,)),
            dma((3,)),
            dma((3, 2)),
            dma((3, 2)),
            dma((2, 3, 2)),
            dma((2, 3, 2)),
            dma((2, NCHUNK)),
            dma((2, NCHUNK)),
            dma((2, NCHUNK)),
            dma((2, NCHUNK)),
            dma((NCHUNK,)),
            dma((NCHUNK,)),
        ],
        compiler_params=pltpu.CompilerParams(
            collective_id=0, has_side_effects=True, vmem_limit_bytes=60 * 2**20
        ),
        cost_estimate=pl.CostEstimate(flops=10**10, bytes_accessed=8 * 2**20, transcendentals=8 * 2**20),
    )(queries, keys, values, out_weight)


def solution(mesh):
    in_specs = (P("seq", "kvh"), P("seq", "kvh"), P("seq", "kvh"), P("kvh", None))
    out_specs = (P("seq", "kvh"), P("kvh", "seq"))
    return jax.shard_map(body, mesh=mesh, in_specs=in_specs, out_specs=out_specs, check_vma=False)
```
